32 devices in a mesh: parts: 2 (over x), row: 16 (over z, y, core).
Axes of the slice: x: 2, y: 2, z: 4, core: 2. Of those that a mesh axis runs over, the one named last changes fastest.
Arguments:
- solid_points: float32 [768, 3, 256], P(('parts', 'row')), parts along dimension 0
- solid_counts: int32 [768], P(('parts', 'row')), parts along dimension 0, may hold values from 64 to 256, as said below
- fluid_points: float32 [1536, 3, 256], P(('parts', 'row')), parts along dimension 0
- fluid_forces: float32 [1536, 3, 256], P(('parts', 'row')), parts along dimension 0
- fluid_counts: int32 [1536], P(('parts', 'row')), parts along dimension 0, may hold values from 64 to 256, as said below
- ss_pairs: int32 [768, 9], P(('parts', 'row')), parts along dimension 0, may hold values from -1 to 383, as said below
- sf_pairs: int32 [768, 18], P(('parts', 'row')), parts along dimension 0, may hold values from -1 to 767, as said below
Outputs:
- mapped_forces: float32 [768, 3, 256], P(('parts', 'row')), parts along dimension 0
- residual: float32 [768, 3, 256], P(('parts', 'row')), parts along dimension 0
The draws below stay inside these ranges and needn't reach their ends.
There are 2 independent parts, one for each index of `parts`. The reference program is written for one: setup_inputs(seed, part) draws one part's arguments, and reference() takes and returns one part's arrays. A program takes and returns all parts, laid end to end along the dimension named above; each array names one. Nothing has to cross between parts.
Inputs may be any that keep to these rules, and one draw needn't show every extreme that they name: The first solid_counts[b] vertex slots of box b hold its vertices; the others are padding. The first fluid_counts[f] vertex slots of box f hold its vertices; the others are padding. `ss_pairs`: row b begins with b itself, then solid boxes paired with b, each between b - 24 and b + 24 and none twice, in some order, then -1 in the unused slots. Box e is listed in row b exactly when b is listed in row e. Some row has all 9 slots live. `sf_pairs`: row b begins with 2 b and 2 b + 1, then other fluid boxes paired with solid box b, each between 2 b - 48 and 2 b + 2 * 24 + 1 and none twice, in some order, then -1 in the unused slots. Some row has all 18 slots live.
All inputs are finite; a program needn't handle non-finite values.
Results may differ from the reference program's by a relative error of at most 0.0003.
Values sent between devices are 32-bit elements; how exact they have to be, the bound alone decides.
A program may use at most 64 MiB of HBM per device.

```python
import math
import jax
import jax.numpy as jnp
from jax import lax

BOX = 256
SB_DEV = 24
ITERS = 2
STRIP = 23
NSB = 384
NFB = 768
N_ROW = 16


def surface_points(key, boxes_total, columns, cell_width, power):
    box_ids = jnp.arange(boxes_total, dtype=jnp.int32)
    column_pos = (box_ids % columns).astype(jnp.float32)
    strip_pos = (box_ids // columns).astype(jnp.float32)
    unit_draw = jax.random.uniform(key, (boxes_total, 3, BOX), jnp.float32) ** power
    coord_x = (column_pos[:, None] + unit_draw[:, 0]) * cell_width
    coord_y = strip_pos[:, None] + unit_draw[:, 1]
    coord_z = 0.2 * unit_draw[:, 2] - 0.1
    return jnp.stack([coord_x, coord_y, coord_z], axis=1)


def draw_solid_points(key, part):
    key = jax.random.fold_in(key, 11)
    power = 1.0
    return surface_points(key, NSB, STRIP, 1.0, power)


def draw_fluid_points(key, part):
    key = jax.random.fold_in(key, 12)
    power = 1.0
    return surface_points(key, NFB, 2 * STRIP, 0.5, power)


def draw_fluid_forces(key, part):
    key = jax.random.fold_in(key, 13)
    key_scale, key_value = jax.random.split(key)
    box_ids = jnp.arange(NFB, dtype=jnp.int32).astype(jnp.float32)
    box_scale = jnp.exp(jax.random.uniform(key_scale, (NFB,), jnp.float32) * math.log(10.0))
    box_scale = box_scale * jnp.power(3.0, box_ids / NFB)
    base = jax.random.normal(key_value, (NFB, 3, BOX), jnp.float32)
    return base * box_scale[:, None, None]


def valid_counts(key, boxes_total):
    counts = jax.random.randint(key, (boxes_total,), BOX // 4, BOX + 1)
    return counts.at[0].set(BOX).at[1].set(BOX // 4).astype(jnp.int32)


def draw_solid_counts(key, part):
    key = jax.random.fold_in(key, 14)
    return valid_counts(key, NSB)


def draw_fluid_counts(key, part):
    key = jax.random.fold_in(key, 15)
    return valid_counts(key, NFB)


def partner_list(key, candidates, valid):
    width_cand = candidates.shape[1]
    scores = jax.random.randint(key, candidates.shape, 0, 4096) * 16 + jnp.arange(width_cand, dtype=jnp.int32)[None, :]
    scores = jnp.where(valid, scores, scores + 262144)
    order = jnp.argsort(scores, axis=1, stable=True)
    chosen = jnp.take_along_axis(candidates, order, axis=1)
    live_total = jnp.sum(valid.astype(jnp.int32), axis=1)
    slot_ids = jnp.arange(width_cand, dtype=jnp.int32)
    return jnp.where(slot_ids[None, :] < live_total[:, None], chosen, -1).astype(jnp.int32)


def draw_ss_pairs(key, part):
    key = jax.random.fold_in(key, 16)
    key_order, key_keep = jax.random.split(key)
    box_ids = jnp.arange(NSB, dtype=jnp.int32)
    column_ids = box_ids % STRIP
    step_x = jnp.array([1, -1, 0, 0, 1, -1, 1, -1], jnp.int32)
    step_y = jnp.array([0, 0, 1, -1, 1, -1, -1, 1], jnp.int32)
    candidates = box_ids[:, None] + step_y[None, :] * STRIP + step_x[None, :]
    moved_col = column_ids[:, None] + step_x[None, :]
    valid = (moved_col >= 0) & (moved_col < STRIP) & (candidates >= 0) & (candidates < NSB)
    center = STRIP + 1
    keep_edge = jax.random.randint(key_keep, (NSB, 4), 0, 4) > 0
    forced = (box_ids >= center - STRIP - 1) & (box_ids <= center + STRIP + 1)
    keep_edge = keep_edge | forced[:, None]
    slot_ids = jnp.arange(8, dtype=jnp.int32)
    edge_kind = slot_ids // 2
    forward = slot_ids % 2 == 0
    owner = jnp.where(forward[None, :], box_ids[:, None], jnp.clip(candidates, 0, NSB - 1))
    kept = keep_edge[owner, edge_kind[None, :]]
    chosen = partner_list(key_order, candidates, valid & kept)
    return jnp.concatenate([box_ids[:, None], chosen], axis=1).astype(jnp.int32)


def draw_sf_pairs(key, part):
    key = jax.random.fold_in(key, 17)
    key_order, key_keep = jax.random.split(key)
    fluid_strip = 2 * STRIP
    box_ids = jnp.arange(NSB, dtype=jnp.int32)
    base_ids = 2 * box_ids
    base_col = 2 * (box_ids % STRIP)
    step_x = jnp.array([-2, -1, 2, 3, -2, -1, 0, 1, 2, 3, -2, -1, 0, 1, 2, 3], jnp.int32)
    step_y = jnp.array([0, 0, 0, 0, 1, 1, 1, 1, 1, 1, -1, -1, -1, -1, -1, -1], jnp.int32)
    candidates = base_ids[:, None] + step_y[None, :] * fluid_strip + step_x[None, :]
    moved_col = base_col[:, None] + step_x[None, :]
    valid = (moved_col >= 0) & (moved_col < fluid_strip) & (candidates >= 0) & (candidates < NFB)
    keep_slot = jax.random.randint(key_keep, candidates.shape, 0, 4) > 0
    keep_slot = keep_slot | (box_ids == STRIP + 1)[:, None]
    chosen = partner_list(key_order, candidates, valid & keep_slot)
    return jnp.concatenate([base_ids[:, None], base_ids[:, None] + 1, chosen], axis=1).astype(jnp.int32)


def setup_inputs(seed: int = 0, part: int = 0) -> dict:
    keys = jax.random.split(jax.random.key(seed), 8)
    part_keys = jax.random.split(jax.random.fold_in(keys[7], part), 8)
    return {
        "solid_points": draw_solid_points(jax.random.fold_in(jax.random.fold_in(keys[7], part), 71), part),
        "solid_counts": draw_solid_counts(jax.random.fold_in(jax.random.fold_in(keys[7], part), 71), part),
        "fluid_points": draw_fluid_points(jax.random.fold_in(jax.random.fold_in(keys[7], part), 71), part),
        "fluid_forces": draw_fluid_forces(jax.random.fold_in(jax.random.fold_in(keys[7], part), 71), part),
        "fluid_counts": draw_fluid_counts(jax.random.fold_in(jax.random.fold_in(keys[7], part), 71), part),
        "ss_pairs": draw_ss_pairs(jax.random.fold_in(jax.random.fold_in(keys[7], part), 71), part),
        "sf_pairs": draw_sf_pairs(jax.random.fold_in(jax.random.fold_in(keys[7], part), 71), part),
    }


RADIUS = 0.9
DIAGONAL_SHIFT = 0.5

def distances(points, others):
    along_x = points[:, 0, :, None] - others[:, 0, None, :]
    along_y = points[:, 1, :, None] - others[:, 1, None, :]
    along_z = points[:, 2, :, None] - others[:, 2, None, :]
    return along_x * along_x + along_y * along_y + along_z * along_z

def wendland(squared):
    scaled = jnp.sqrt(squared) / RADIUS
    falling = jnp.maximum(1.0 - scaled, 0.0)
    return falling * falling * falling * falling * (4.0 * scaled + 1.0)

def pair_terms(points, others, values, pair_ids, offset, slot_limit):

    def add_slot(slot_index, running):
        column = lax.dynamic_index_in_dim(pair_ids, slot_index, 1, keepdims=False)
        live_mask = column >= 0
        position = jnp.where(live_mask, column - offset, 0)
        nearby = jnp.take(others, position, axis=0)
        carried = jnp.where(live_mask[:, None, None], jnp.take(values, position, axis=0), 0.0)
        kernel = wendland(distances(points, nearby))
        return running + jnp.einsum('sij,scj->sci', kernel, carried, precision=lax.Precision.HIGHEST)
    zeros_init = jnp.zeros((points.shape[0], 3, points.shape[2]), jnp.float32)
    return lax.fori_loop(0, slot_limit, add_slot, zeros_init)

def blocked_terms(points, others, values, pair_ids):
    shaped_points = points.reshape(N_ROW, SB_DEV, 3, BOX)
    shaped_pairs = pair_ids.reshape(N_ROW, SB_DEV, pair_ids.shape[1])

    def one_block(member):
        return pair_terms(member[0], others, values, member[1], 0, member[1].shape[1])
    return lax.map(one_block, (shaped_points, shaped_pairs)).reshape(points.shape)

def lane_mask(counts, box_width):
    lane_ids = jnp.arange(box_width, dtype=jnp.int32)
    return (lane_ids[None, :] < counts[:, None]).astype(jnp.float32)[:, None, :]

def per_component(first_field, second_field):
    return lax.optimization_barrier(jnp.sum(first_field * second_field, axis=(0, 2)))

def expand(factor):
    return factor[None, :, None]

def reference(solid_points, solid_counts, fluid_points, fluid_forces, fluid_counts, ss_pairs, sf_pairs):
    solid_mask = lane_mask(solid_counts, BOX)
    fluid_loads = fluid_forces * lane_mask(fluid_counts, BOX)
    mapped = blocked_terms(solid_points, fluid_points, fluid_loads, sf_pairs)
    right_side = solid_mask * (mapped * (1.0 / math.sqrt(BOX)))

    def operate(vector):
        image = blocked_terms(solid_points, solid_points, vector, ss_pairs)
        return solid_mask * (image / BOX) + DIAGONAL_SHIFT * vector
    solution = jnp.zeros_like(right_side)
    residual = right_side
    direction = right_side
    norm_now = per_component(residual, residual)
    for iteration in range(ITERS):
        image = operate(direction)
        step_size = expand(norm_now / per_component(direction, image))
        solution = solution + step_size * direction
        residual = residual - step_size * image
        if iteration + 1 < ITERS:
            norm_next = per_component(residual, residual)
            direction = residual + expand(norm_next / norm_now) * direction
            norm_now = norm_next
    return (solution, residual)
```

```python
import functools
import math

import jax
import jax.numpy as jnp
from jax import lax
from jax.experimental import pallas as pl
from jax.experimental.pallas import tpu as pltpu
from jax.sharding import PartitionSpec as P

RADIUS = 0.9
DIAGONAL_SHIFT = 0.5
PHI_SCALE = 4.0 / RADIUS**5
CHUNK = 64
STEP = 32
VMEM_BYTES = 50 * 1024 * 1024
F32 = jnp.float32
BF16 = jnp.bfloat16


def vmem():
    return pl.BlockSpec(memory_space=pltpu.VMEM)


def anywhere():
    return pl.BlockSpec(memory_space=pl.ANY)


def greet(targets):
    barrier = pltpu.get_barrier_semaphore()
    for target in targets:
        pl.semaphore_signal(
            barrier, inc=1, device_id={"row": target}, device_id_type=pl.DeviceIdType.MESH
        )
    pl.semaphore_wait(barrier, len(targets))


def send(src, dst, send_sem, recv_sem, target):
    copy = pltpu.make_async_remote_copy(
        src_ref=src,
        dst_ref=dst,
        send_sem=send_sem,
        recv_sem=recv_sem,
        device_id={"row": target},
        device_id_type=pl.DeviceIdType.MESH,
    )
    copy.start()
    return copy


def halo_kernel(devices, total, *refs):
    sources, exts = refs[:total], refs[total : 2 * total]
    send_sems, recv_sems, own_sems = refs[2 * total :]
    me = lax.axis_index("row")
    right = lax.rem(me + 1, devices)
    left = lax.rem(me + devices - 1, devices)
    own = []
    for k in range(total):
        copy = pltpu.make_async_copy(sources[k], exts[k].at[1], own_sems.at[k])
        copy.start()
        own.append(copy)
    greet([left, right])
    copies = []
    for k in range(total):
        copies.append(
            send(sources[k], exts[k].at[0], send_sems.at[2 * k], recv_sems.at[2 * k], right)
        )
        copies.append(
            send(sources[k], exts[k].at[2], send_sems.at[2 * k + 1], recv_sems.at[2 * k + 1], left)
        )
    for copy in own:
        copy.wait()
    for copy in copies:
        copy.wait()


def with_halo(arrays, devices, collective_id):
    total = len(arrays)
    outs = pl.pallas_call(
        functools.partial(halo_kernel, devices, total),
        out_shape=[jax.ShapeDtypeStruct((3,) + a.shape, a.dtype) for a in arrays],
        in_specs=[anywhere()] * total,
        out_specs=[anywhere()] * total,
        scratch_shapes=[
            pltpu.SemaphoreType.DMA((2 * total,)),
            pltpu.SemaphoreType.DMA((2 * total,)),
            pltpu.SemaphoreType.DMA((total,)),
        ],
        compiler_params=pltpu.CompilerParams(collective_id=collective_id, has_side_effects=True),
    )(*arrays)
    return outs


def stack_rows(ref, box, width):
    rows = lax.broadcasted_iota(jnp.int32, (8, width), 0)
    stacked = jnp.zeros((8, width), F32)
    for k in range(3):
        row = jnp.broadcast_to(ref[box, pl.ds(k, 1), :], (8, width))
        stacked = jnp.where(rows == k, row, stacked)
    return stacked


def pair_kernel(
    boxes, nearby, slots, width, scale, shift,
    ids, live, own_counts, near_counts,
    own_points, near_points, near_values, *rest,
):
    if shift:
        own_values, out, columns, loads, high, low, acc = rest
    else:
        out, columns, loads, high, low, acc = rest
    lanes = lax.broadcasted_iota(jnp.int32, (8, width), 1)

    def prepare(box, carry):
        columns[box, :, 0:8] = stack_rows(near_points, box, width).T
        value = jnp.where(lanes < near_counts[box], stack_rows(near_values, box, width), 0.0)
        top = value.astype(BF16).astype(F32)
        loads[box] = jnp.concatenate([top, value - top], axis=0).astype(BF16)
        return carry

    lax.fori_loop(0, nearby, prepare, 0)
    loads[nearby] = jnp.zeros((16, width), BF16)
    high[...] = jnp.zeros_like(high)
    low[...] = jnp.zeros_like(low)
    acc[...] = jnp.zeros_like(acc)

    def add_pair(box, near, slot):
        value = loads[near]
        total = jnp.dot(value, high[slot], preferred_element_type=F32)
        total = total + jnp.dot(value, low[slot], preferred_element_type=F32)
        acc[box] += total

    def one_box(box, carry):
        wide = own_counts[box] > width // 2

        def one_slot(s, state):
            last_box, last_near, slot = state
            near = ids[box * slots + s]
            chunks = (near_counts[near] + (CHUNK - 1)) // CHUNK

            def variant(rows, span):
                add_pair(last_box, last_near, 1 - slot)
                points = [own_points[box, pl.ds(k, 1), 0:span] for k in range(3)]
                for j in range(0, rows, STEP):
                    squared = None
                    block = columns[near, j : j + STEP, 0:8]
                    for k in range(3):
                        along = block[:, k : k + 1] - points[k]
                        squared = along * along if squared is None else squared + along * along
                    squared = jnp.maximum(squared, 1e-30)
                    distance = squared * lax.rsqrt(squared)
                    falling = jnp.maximum(RADIUS - distance, 0.0)
                    falling = falling * falling
                    phi = falling * falling * (distance + 0.25 * RADIUS)
                    top = phi.astype(BF16)
                    high[slot, j : j + STEP, 0:span] = top
                    low[slot, j : j + STEP, 0:span] = (phi - top.astype(F32)).astype(BF16)

            for count in range(1, width // CHUNK + 1):
                for span in (width // 2, width):
                    is_wide = span == width

                    @pl.when(jnp.logical_and(chunks == count, wide == is_wide))
                    def _(count=count, span=span):
                        variant(count * CHUNK, span)

            return box, near, 1 - slot

        return lax.fori_loop(0, live[box], one_slot, carry)

    last_box, last_near, slot = lax.fori_loop(
        0, boxes, one_box, (jnp.int32(0), jnp.int32(nearby), jnp.int32(0))
    )
    add_pair(last_box, last_near, 1 - slot)

    def finish(box, carry):
        total = (acc[box, 0:8, :] + acc[box, 8:16, :]) * scale
        total = jnp.where(lanes < own_counts[box], total, 0.0)[0:3]
        if shift:
            total = total + shift * own_values[box]
        out[box] = total
        return carry

    lax.fori_loop(0, boxes, finish, 0)


def pair_terms(ids, live, own_counts, near_counts, own_points, near_points, near_values, scale, shift, own_values=None):
    boxes, slots = ids.shape
    nearby = near_points.shape[0]
    width = own_points.shape[2]
    operands = [own_points, near_points, near_values] + ([own_values] if shift else [])
    smem = pl.BlockSpec(memory_space=pltpu.SMEM)
    work = boxes * slots * width * width
    return pl.pallas_call(
        functools.partial(pair_kernel, boxes, nearby, slots, width, scale, shift),
        out_shape=jax.ShapeDtypeStruct((boxes, 3, width), F32),
        in_specs=[smem] * 4 + [vmem()] * len(operands),
        out_specs=vmem(),
        scratch_shapes=[
            pltpu.VMEM((nearby, width, 128), F32),
            pltpu.VMEM((nearby + 1, 16, width), BF16),
            pltpu.VMEM((2, width, width), BF16),
            pltpu.VMEM((2, width, width), BF16),
            pltpu.VMEM((boxes, 16, width), F32),
        ],
        compiler_params=pltpu.CompilerParams(vmem_limit_bytes=VMEM_BYTES),
        cost_estimate=pl.CostEstimate(flops=20 * work, bytes_accessed=1 << 20, transcendentals=work),
    )(ids.reshape(-1), live, own_counts, near_counts, *operands)


def lane_parts(first, second):
    total = jnp.sum(first * second, axis=0)
    half = total.shape[1] // 2
    return total[:, :half] + total[:, half:]


def gather_sums(devices, gathered, send_sems, recv_sems, me, base):
    copies = []
    for step in range(1, devices):
        target = lax.rem(me + step, devices)
        copies.append(
            send(
                gathered.at[me],
                gathered.at[me],
                send_sems.at[base + step],
                recv_sems.at[base + step],
                target,
            )
        )
    return copies


def whole_sum(gathered, first):
    rows = jnp.sum(gathered[:, first : first + 3, :], axis=0)
    return jnp.sum(rows, axis=1, keepdims=True)


def first_kernel(devices, rhs, image, direction, coefs, landed, gathered, send_sems, recv_sems):
    me = lax.axis_index("row")
    right = lax.rem(me + 1, devices)
    left = lax.rem(me + devices - 1, devices)
    base = rhs[1]
    mine = image[...]
    gathered[me] = jnp.zeros(gathered.shape[1:], F32)
    gathered[me, 0:3] = lane_parts(base, base)
    gathered[me, 3:6] = lane_parts(base, mine)
    gathered[me, 6:9] = lane_parts(mine, mine)
    greet([lax.rem(me + step, devices) for step in range(1, devices)])
    copies = gather_sums(devices, gathered, send_sems, recv_sems, me, 1)
    copies.append(send(image, landed.at[0], send_sems.at[0], recv_sems.at[0], right))
    copies.append(send(image, landed.at[1], send_sems.at[1], recv_sems.at[1], left))
    for copy in copies:
        copy.wait()
    norm = whole_sum(gathered, 0)
    alpha = norm / whole_sum(gathered, 3)
    norm_next = norm - 2.0 * alpha * whole_sum(gathered, 3) + alpha * alpha * whole_sum(gathered, 6)
    beta = norm_next / norm
    coefs[...] = jnp.zeros_like(coefs)
    coefs[0:3] = jnp.broadcast_to(alpha, (3, coefs.shape[1]))
    coefs[3:6] = jnp.broadcast_to(norm_next, (3, coefs.shape[1]))
    direction[0] = (rhs[0] - alpha[None] * landed[0]) + beta[None] * rhs[0]
    direction[1] = (base - alpha[None] * mine) + beta[None] * base
    direction[2] = (rhs[2] - alpha[None] * landed[1]) + beta[None] * rhs[2]


def last_kernel(devices, rhs, image, direction, second, coefs, mapped, residual, gathered, send_sems, recv_sems):
    me = lax.axis_index("row")
    base = rhs[1]
    along = direction[1]
    gathered[me] = jnp.zeros(gathered.shape[1:], F32)
    gathered[me, 0:3] = lane_parts(along, second[...])
    greet([lax.rem(me + step, devices) for step in range(1, devices)])
    for copy in gather_sums(devices, gathered, send_sems, recv_sems, me, -1):
        copy.wait()
    alpha = coefs[0:3, 0:1][None]
    alpha_next = (coefs[3:6, 0:1] / whole_sum(gathered, 0))[None]
    mapped[...] = alpha * base + alpha_next * along
    residual[...] = (base - alpha * image[...]) - alpha_next * second[...]


def body(solid_points, solid_counts, fluid_points, fluid_forces, fluid_counts, ss_pairs, sf_pairs):
    boxes, _, width = solid_points.shape
    fluids = fluid_points.shape[0]
    devices = lax.axis_size("row")
    me = lax.axis_index("row")
    count_lanes = -(-max(boxes, fluids) // 128) * 128
    counts = jnp.zeros((8, count_lanes), jnp.int32)
    counts = counts.at[0, :fluids].set(fluid_counts).at[1, :boxes].set(solid_counts)
    near_solid, near_fluid, near_forces, near_counts = with_halo(
        [solid_points, fluid_points, fluid_forces, counts], devices, 0
    )
    near_fluid = near_fluid.reshape(3 * fluids, 3, width)
    near_forces = near_forces.reshape(3 * fluids, 3, width)
    near_solid = near_solid.reshape(3 * boxes, 3, width)
    near_fluid_counts = near_counts[:, 0, :fluids].reshape(-1)
    near_solid_counts = near_counts[:, 1, :boxes].reshape(-1)
    sf_live = jnp.sum((sf_pairs >= 0).astype(jnp.int32), axis=1)
    ss_live = jnp.sum((ss_pairs >= 0).astype(jnp.int32), axis=1)
    sf_ids = jnp.clip(sf_pairs - (me - 1) * fluids, 0, 3 * fluids - 1)
    ss_ids = jnp.clip(ss_pairs - (me - 1) * boxes, 0, 3 * boxes - 1)

    rhs = pair_terms(
        sf_ids, sf_live, solid_counts, near_fluid_counts,
        solid_points, near_fluid, near_forces,
        PHI_SCALE / math.sqrt(width), 0.0,
    )
    (near_rhs,) = with_halo([rhs], devices, 1)

    def operate(near, own):
        return pair_terms(
            ss_ids, ss_live, solid_counts, near_solid_counts,
            solid_points, near_solid, near.reshape(3 * boxes, 3, width),
            PHI_SCALE / width, DIAGONAL_SHIFT, own,
        )

    image = operate(near_rhs, rhs)
    block = jax.ShapeDtypeStruct((boxes, 3, width), F32)
    direction, coefs = pl.pallas_call(
        functools.partial(first_kernel, devices),
        out_shape=[
            jax.ShapeDtypeStruct((3, boxes, 3, width), F32),
            jax.ShapeDtypeStruct((8, 128), F32),
        ],
        in_specs=[vmem()] * 2,
        out_specs=[vmem()] * 2,
        scratch_shapes=[
            pltpu.VMEM((2, boxes, 3, width), F32),
            pltpu.VMEM((devices, 16, width // 2), F32),
            pltpu.SemaphoreType.DMA((devices + 1,)),
            pltpu.SemaphoreType.DMA((devices + 1,)),
        ],
        compiler_params=pltpu.CompilerParams(collective_id=2, has_side_effects=True),
    )(near_rhs, image)
    second = operate(direction, direction[1])
    return tuple(
        pl.pallas_call(
            functools.partial(last_kernel, devices),
            out_shape=[block, block],
            in_specs=[vmem()] * 5,
            out_specs=[vmem()] * 2,
            scratch_shapes=[
                pltpu.VMEM((devices, 16, width // 2), F32),
                pltpu.SemaphoreType.DMA((devices - 1,)),
                pltpu.SemaphoreType.DMA((devices - 1,)),
            ],
            compiler_params=pltpu.CompilerParams(collective_id=3, has_side_effects=True),
        )(near_rhs, image, direction, second, coefs)
    )


def solution(mesh):
    return jax.shard_map(
        body,
        mesh=mesh,
        in_specs=(
            P(("parts", "row"), None, None),
            P(("parts", "row")),
            P(("parts", "row"), None, None),
            P(("parts", "row"), None, None),
            P(("parts", "row")),
            P(("parts", "row"), None),
            P(("parts", "row"), None),
        ),
        out_specs=(P(("parts", "row"), None, None), P(("parts", "row"), None, None)),
        check_vma=False,
    )
```

```python
import functools
import math

import jax
import jax.numpy as jnp
from jax import lax
from jax.experimental import pallas as pl
from jax.experimental.pallas import tpu as pltpu
from jax.sharding import PartitionSpec as P

RADIUS = 0.9
DIAGONAL_SHIFT = 0.5
PHI_SCALE = 4.0 / RADIUS**5
CHUNK = 32
GROUP = 4
LANES = 128
STEP = 32
VMEM_BYTES = 32 * 1024 * 1024
F32 = jnp.float32
BF16 = jnp.bfloat16


def vmem():
    return pl.BlockSpec(memory_space=pltpu.VMEM)


def anywhere():
    return pl.BlockSpec(memory_space=pl.ANY)


def greet(targets):
    barrier = pltpu.get_barrier_semaphore()
    for target in targets:
        pl.semaphore_signal(
            barrier, inc=1, device_id={"row": target}, device_id_type=pl.DeviceIdType.MESH
        )
    pl.semaphore_wait(barrier, len(targets))


def send(src, dst, send_sem, recv_sem, target):
    copy = pltpu.make_async_remote_copy(
        src_ref=src,
        dst_ref=dst,
        send_sem=send_sem,
        recv_sem=recv_sem,
        device_id={"row": target},
        device_id_type=pl.DeviceIdType.MESH,
    )
    copy.start()
    return copy


def halo_kernel(devices, total, *refs):
    sources, exts = refs[:total], refs[total : 2 * total]
    send_sems, recv_sems, own_sems = refs[2 * total :]
    me = lax.axis_index("row")
    right = lax.rem(me + 1, devices)
    left = lax.rem(me + devices - 1, devices)
    own = []
    for k in range(total):
        copy = pltpu.make_async_copy(sources[k], exts[k].at[1], own_sems.at[k])
        copy.start()
        own.append(copy)
    greet([left, right])
    copies = []
    for k in range(total):
        copies.append(
            send(sources[k], exts[k].at[0], send_sems.at[2 * k], recv_sems.at[2 * k], right)
        )
        copies.append(
            send(sources[k], exts[k].at[2], send_sems.at[2 * k + 1], recv_sems.at[2 * k + 1], left)
        )
    for copy in own:
        copy.wait()
    for copy in copies:
        copy.wait()


def with_halo(arrays, devices, collective_id):
    total = len(arrays)
    outs = pl.pallas_call(
        functools.partial(halo_kernel, devices, total),
        out_shape=[jax.ShapeDtypeStruct((3,) + a.shape, a.dtype) for a in arrays],
        in_specs=[anywhere()] * total,
        out_specs=[anywhere()] * total,
        scratch_shapes=[
            pltpu.SemaphoreType.DMA((2 * total,)),
            pltpu.SemaphoreType.DMA((2 * total,)),
            pltpu.SemaphoreType.DMA((total,)),
        ],
        compiler_params=pltpu.CompilerParams(collective_id=collective_id, has_side_effects=True),
    )(*arrays)
    return outs


def stack_rows(ref, box, width):
    rows = lax.broadcasted_iota(jnp.int32, (8, width), 0)
    stacked = jnp.zeros((8, width), F32)
    for k in range(3):
        row = jnp.broadcast_to(ref[box, pl.ds(k, 1), :], (8, width))
        stacked = jnp.where(rows == k, row, stacked)
    return stacked


def pair_kernel(
    boxes, nearby, slots, width, scale, shift,
    load_ids, point_ids, groups, own_counts, near_counts,
    own_points, near_points, near_values, *rest,
):
    if shift:
        own_values, out, columns, loads, high, low, acc = rest
    else:
        out, columns, loads, high, low, acc = rest
    lanes = lax.broadcasted_iota(jnp.int32, (8, width), 1)

    def prepare(box, carry):
        value = jnp.where(lanes < near_counts[box], stack_rows(near_values, box, width), 0.0)
        top = value.astype(BF16).astype(F32)
        middle = (value - top).astype(BF16).astype(F32)
        terms = [top, middle, value - top - middle, jnp.zeros_like(value)]
        terms = jnp.concatenate(terms, axis=0).astype(BF16)
        loads[2 * box + 1] = terms[:, :LANES]
        loads[2 * box + 2] = terms[:, LANES:]
        return carry

    lax.fori_loop(0, nearby, prepare, 0, unroll=8)
    loads[0] = jnp.zeros(loads.shape[1:], BF16)
    high[...] = jnp.zeros_like(high)
    low[...] = jnp.zeros_like(low)

    def box_rows(box, rows):
        turned = stack_rows(own_points, box, width).T[0:rows]
        for k in range(3):
            columns[k, 0:rows, :] = jnp.broadcast_to(turned[:, k : k + 1], (rows, LANES))
        acc[...] = jnp.zeros_like(acc)

        def add_group(units, slot):
            value = jnp.concatenate([loads[unit] for unit in units], axis=1)
            total = None
            for part in (high, low):
                term = lax.dot_general(
                    value, part[slot, 0:rows, :], (((1,), (1,)), ((), ())),
                    preferred_element_type=F32,
                )
                total = term if total is None else total + term
            acc[:, 0:rows] += total

        def one_group(g, state):
            slot = state[0]
            add_group(state[1:], 1 - slot)
            first = box * slots + g * GROUP
            points = []
            for unit in range(GROUP):
                place = point_ids[first + unit]
                near = place // 2
                lane = pl.multiple_of((place % 2) * LANES, LANES)
                points.append(
                    [near_points[near, pl.ds(k, 1), pl.ds(lane, LANES)] for k in range(3)]
                )
            for j in range(0, rows, STEP):
                own = [columns[k, j : j + STEP, :] for k in range(3)]
                for unit in range(GROUP):
                    squared = None
                    for k in range(3):
                        along = own[k] - points[unit][k]
                        squared = along * along if squared is None else squared + along * along
                    squared = jnp.maximum(squared, 1e-30)
                    distance = squared * lax.rsqrt(squared)
                    falling = jnp.maximum(RADIUS - distance, 0.0)
                    falling = falling * falling
                    phi = falling * falling * (distance + 0.25 * RADIUS)
                    top = phi.astype(BF16)
                    where = pl.ds(unit * LANES, LANES)
                    high[slot, j : j + STEP, where] = top
                    low[slot, j : j + STEP, where] = (phi - top.astype(F32)).astype(BF16)
            return (1 - slot,) + tuple(load_ids[first + unit] for unit in range(GROUP))

        zero = jnp.int32(0)
        state = lax.fori_loop(0, groups[box], one_group, (zero,) * (GROUP + 1))
        add_group(state[1:], 1 - state[0])
        total = (acc[0:8] + (acc[8:16] + acc[16:24])) * scale
        total = jnp.where(lanes < own_counts[box], total, 0.0)[0:3]
        if shift:
            total = total + shift * own_values[box]
        out[box] = total

    def one_box(box, carry):
        chunks = jnp.maximum((own_counts[box] + (CHUNK - 1)) // CHUNK, 2)
        for count in range(2, width // CHUNK + 1):

            @pl.when(chunks == count)
            def _(count=count):
                box_rows(box, count * CHUNK)

        return carry

    lax.fori_loop(0, boxes, one_box, 0)


def unit_lists(ids, live, near_counts):
    boxes, slots = ids.shape
    nearby = near_counts.shape[0]
    chosen = ids[:, :, None] == jnp.arange(nearby, dtype=jnp.int32)
    counts = jnp.sum(jnp.where(chosen, near_counts, 0), axis=2)
    used = jnp.arange(slots, dtype=jnp.int32)[None] < live[:, None]
    flags = jnp.stack([used, used & (counts > LANES)], axis=2).reshape(boxes, 2 * slots)
    units = jnp.stack([2 * ids + 1, 2 * ids + 2], axis=2).reshape(boxes, 2 * slots)
    entry = jnp.arange(2 * slots, dtype=jnp.int32)
    before = flags[:, None, :] & (entry[None, :] < entry[:, None])[None]
    place = jnp.where(flags, jnp.sum(before.astype(jnp.int32), axis=2), -1)
    length = -(-2 * slots // GROUP) * GROUP
    target = place[:, None, :] == jnp.arange(length, dtype=jnp.int32)[None, :, None]
    load_ids = jnp.sum(jnp.where(target, units[:, None, :], 0), axis=2)
    point_ids = jnp.where(load_ids > 0, load_ids, load_ids[:, :1]) - 1
    total = jnp.sum(flags.astype(jnp.int32), axis=1)
    return load_ids, point_ids, (total + (GROUP - 1)) // GROUP


def pair_terms(ids, live, own_counts, near_counts, own_points, near_points, near_values, scale, shift, own_values=None):
    boxes, slots = ids.shape
    nearby = near_points.shape[0]
    width = own_points.shape[2]
    operands = [own_points, near_points, near_values] + ([own_values] if shift else [])
    smem = pl.BlockSpec(memory_space=pltpu.SMEM)
    work = boxes * slots * width * width
    load_ids, point_ids, groups = unit_lists(ids, live, near_counts)
    return pl.pallas_call(
        functools.partial(
            pair_kernel, boxes, nearby, load_ids.shape[1], width, scale, shift
        ),
        out_shape=jax.ShapeDtypeStruct((boxes, 3, width), F32),
        in_specs=[smem] * 5 + [vmem()] * len(operands),
        out_specs=vmem(),
        scratch_shapes=[
            pltpu.VMEM((3, width, LANES), F32),
            pltpu.VMEM((2 * nearby + 1, 32, LANES), BF16),
            pltpu.VMEM((2, width, GROUP * LANES), BF16),
            pltpu.VMEM((2, width, GROUP * LANES), BF16),
            pltpu.VMEM((32, width), F32),
        ],
        compiler_params=pltpu.CompilerParams(vmem_limit_bytes=VMEM_BYTES),
        cost_estimate=pl.CostEstimate(flops=20 * work, bytes_accessed=1 << 20, transcendentals=work),
    )(load_ids.reshape(-1), point_ids.reshape(-1), groups, own_counts, near_counts, *operands)


def lane_parts(first, second):
    total = jnp.sum(first * second, axis=0)
    half = total.shape[1] // 2
    return total[:, :half] + total[:, half:]


def gather_sums(devices, gathered, send_sems, recv_sems, me, base):
    copies = []
    for step in range(1, devices):
        target = lax.rem(me + step, devices)
        copies.append(
            send(
                gathered.at[me],
                gathered.at[me],
                send_sems.at[base + step],
                recv_sems.at[base + step],
                target,
            )
        )
    return copies


def whole_sum(gathered, first):
    rows = jnp.sum(gathered[:, first : first + 3, :], axis=0)
    return jnp.sum(rows, axis=1, keepdims=True)


def first_kernel(devices, rhs, image, direction, coefs, landed, gathered, send_sems, recv_sems):
    me = lax.axis_index("row")
    right = lax.rem(me + 1, devices)
    left = lax.rem(me + devices - 1, devices)
    base = rhs[1]
    mine = image[...]
    gathered[me] = jnp.zeros(gathered.shape[1:], F32)
    gathered[me, 0:3] = lane_parts(base, base)
    gathered[me, 3:6] = lane_parts(base, mine)
    gathered[me, 6:9] = lane_parts(mine, mine)
    greet([lax.rem(me + step, devices) for step in range(1, devices)])
    copies = gather_sums(devices, gathered, send_sems, recv_sems, me, 1)
    copies.append(send(image, landed.at[0], send_sems.at[0], recv_sems.at[0], right))
    copies.append(send(image, landed.at[1], send_sems.at[1], recv_sems.at[1], left))
    for copy in copies:
        copy.wait()
    norm = whole_sum(gathered, 0)
    alpha = norm / whole_sum(gathered, 3)
    norm_next = norm - 2.0 * alpha * whole_sum(gathered, 3) + alpha * alpha * whole_sum(gathered, 6)
    beta = norm_next / norm
    coefs[...] = jnp.zeros_like(coefs)
    coefs[0:3] = jnp.broadcast_to(alpha, (3, coefs.shape[1]))
    coefs[3:6] = jnp.broadcast_to(norm_next, (3, coefs.shape[1]))
    direction[0] = (rhs[0] - alpha[None] * landed[0]) + beta[None] * rhs[0]
    direction[1] = (base - alpha[None] * mine) + beta[None] * base
    direction[2] = (rhs[2] - alpha[None] * landed[1]) + beta[None] * rhs[2]


def last_kernel(devices, rhs, image, direction, second, coefs, mapped, residual, gathered, send_sems, recv_sems):
    me = lax.axis_index("row")
    base = rhs[1]
    along = direction[1]
    gathered[me] = jnp.zeros(gathered.shape[1:], F32)
    gathered[me, 0:3] = lane_parts(along, second[...])
    greet([lax.rem(me + step, devices) for step in range(1, devices)])
    for copy in gather_sums(devices, gathered, send_sems, recv_sems, me, -1):
        copy.wait()
    alpha = coefs[0:3, 0:1][None]
    alpha_next = (coefs[3:6, 0:1] / whole_sum(gathered, 0))[None]
    mapped[...] = alpha * base + alpha_next * along
    residual[...] = (base - alpha * image[...]) - alpha_next * second[...]


def body(solid_points, solid_counts, fluid_points, fluid_forces, fluid_counts, ss_pairs, sf_pairs):
    boxes, _, width = solid_points.shape
    fluids = fluid_points.shape[0]
    devices = lax.axis_size("row")
    me = lax.axis_index("row")
    count_lanes = -(-max(boxes, fluids) // 128) * 128
    counts = jnp.zeros((8, count_lanes), jnp.int32)
    counts = counts.at[0, :fluids].set(fluid_counts).at[1, :boxes].set(solid_counts)
    near_solid, near_fluid, near_forces, near_counts = with_halo(
        [solid_points, fluid_points, fluid_forces, counts], devices, 0
    )
    near_fluid = near_fluid.reshape(3 * fluids, 3, width)
    near_forces = near_forces.reshape(3 * fluids, 3, width)
    near_solid = near_solid.reshape(3 * boxes, 3, width)
    near_fluid_counts = near_counts[:, 0, :fluids].reshape(-1)
    near_solid_counts = near_counts[:, 1, :boxes].reshape(-1)
    sf_live = jnp.sum((sf_pairs >= 0).astype(jnp.int32), axis=1)
    ss_live = jnp.sum((ss_pairs >= 0).astype(jnp.int32), axis=1)
    sf_ids = jnp.clip(sf_pairs - (me - 1) * fluids, 0, 3 * fluids - 1)
    ss_ids = jnp.clip(ss_pairs - (me - 1) * boxes, 0, 3 * boxes - 1)

    rhs = pair_terms(
        sf_ids, sf_live, solid_counts, near_fluid_counts,
        solid_points, near_fluid, near_forces,
        PHI_SCALE / math.sqrt(width), 0.0,
    )
    (near_rhs,) = with_halo([rhs], devices, 1)

    def operate(near, own):
        return pair_terms(
            ss_ids, ss_live, solid_counts, near_solid_counts,
            solid_points, near_solid, near.reshape(3 * boxes, 3, width),
            PHI_SCALE / width, DIAGONAL_SHIFT, own,
        )

    image = operate(near_rhs, rhs)
    block = jax.ShapeDtypeStruct((boxes, 3, width), F32)
    direction, coefs = pl.pallas_call(
        functools.partial(first_kernel, devices),
        out_shape=[
            jax.ShapeDtypeStruct((3, boxes, 3, width), F32),
            jax.ShapeDtypeStruct((8, 128), F32),
        ],
        in_specs=[vmem()] * 2,
        out_specs=[vmem()] * 2,
        scratch_shapes=[
            pltpu.VMEM((2, boxes, 3, width), F32),
            pltpu.VMEM((devices, 16, width // 2), F32),
            pltpu.SemaphoreType.DMA((devices + 1,)),
            pltpu.SemaphoreType.DMA((devices + 1,)),
        ],
        compiler_params=pltpu.CompilerParams(collective_id=2, has_side_effects=True),
    )(near_rhs, image)
    second = operate(direction, direction[1])
    return tuple(
        pl.pallas_call(
            functools.partial(last_kernel, devices),
            out_shape=[block, block],
            in_specs=[vmem()] * 5,
            out_specs=[vmem()] * 2,
            scratch_shapes=[
                pltpu.VMEM((devices, 16, width // 2), F32),
                pltpu.SemaphoreType.DMA((devices - 1,)),
                pltpu.SemaphoreType.DMA((devices - 1,)),
            ],
            compiler_params=pltpu.CompilerParams(collective_id=3, has_side_effects=True),
        )(near_rhs, image, direction, second, coefs)
    )


def solution(mesh):
    return jax.shard_map(
        body,
        mesh=mesh,
        in_specs=(
            P(("parts", "row"), None, None),
            P(("parts", "row")),
            P(("parts", "row"), None, None),
            P(("parts", "row"), None, None),
            P(("parts", "row")),
            P(("parts", "row"), None),
            P(("parts", "row"), None),
        ),
        out_specs=(P(("parts", "row"), None, None), P(("parts", "row"), None, None)),
        check_vma=False,
    )
```

```python
import functools
import math

import jax
import jax.numpy as jnp
from jax import lax
from jax.experimental import pallas as pl
from jax.experimental.pallas import tpu as pltpu
from jax.sharding import PartitionSpec as P

RADIUS = 0.9
DIAGONAL_SHIFT = 0.5
PHI_SCALE = 4.0 / RADIUS**5
CHUNK = 32
LANES = 128
STEP = 32
VMEM_BYTES = 32 * 1024 * 1024
F32 = jnp.float32
BF16 = jnp.bfloat16


def vmem():
    return pl.BlockSpec(memory_space=pltpu.VMEM)


def anywhere():
    return pl.BlockSpec(memory_space=pl.ANY)


def greet(targets):
    barrier = pltpu.get_barrier_semaphore()
    for target in targets:
        pl.semaphore_signal(
            barrier, inc=1, device_id={"row": target}, device_id_type=pl.DeviceIdType.MESH
        )
    pl.semaphore_wait(barrier, len(targets))


def send(src, dst, send_sem, recv_sem, target):
    copy = pltpu.make_async_remote_copy(
        src_ref=src,
        dst_ref=dst,
        send_sem=send_sem,
        recv_sem=recv_sem,
        device_id={"row": target},
        device_id_type=pl.DeviceIdType.MESH,
    )
    copy.start()
    return copy


def halo_kernel(devices, total, *refs):
    sources, exts = refs[:total], refs[total : 2 * total]
    send_sems, recv_sems, own_sems = refs[2 * total :]
    me = lax.axis_index("row")
    right = lax.rem(me + 1, devices)
    left = lax.rem(me + devices - 1, devices)
    own = []
    for k in range(total):
        copy = pltpu.make_async_copy(sources[k], exts[k].at[1], own_sems.at[k])
        copy.start()
        own.append(copy)
    greet([left, right])
    copies = []
    for k in range(total):
        copies.append(
            send(sources[k], exts[k].at[0], send_sems.at[2 * k], recv_sems.at[2 * k], right)
        )
        copies.append(
            send(sources[k], exts[k].at[2], send_sems.at[2 * k + 1], recv_sems.at[2 * k + 1], left)
        )
    for copy in own:
        copy.wait()
    for copy in copies:
        copy.wait()


def with_halo(arrays, devices, collective_id):
    total = len(arrays)
    outs = pl.pallas_call(
        functools.partial(halo_kernel, devices, total),
        out_shape=[jax.ShapeDtypeStruct((3,) + a.shape, a.dtype) for a in arrays],
        in_specs=[anywhere()] * total,
        out_specs=[anywhere()] * total,
        scratch_shapes=[
            pltpu.SemaphoreType.DMA((2 * total,)),
            pltpu.SemaphoreType.DMA((2 * total,)),
            pltpu.SemaphoreType.DMA((total,)),
        ],
        compiler_params=pltpu.CompilerParams(collective_id=collective_id, has_side_effects=True),
    )(*arrays)
    return outs


def stack_rows(ref, box, width):
    rows = lax.broadcasted_iota(jnp.int32, (8, width), 0)
    stacked = jnp.zeros((8, width), F32)
    for k in range(3):
        row = jnp.broadcast_to(ref[box, pl.ds(k, 1), :], (8, width))
        stacked = jnp.where(rows == k, row, stacked)
    return stacked


def pair_kernel(
    boxes, nearby, slots, group, width, scale, shift,
    load_ids, point_ids, groups, own_counts, near_counts,
    own_points, near_points, near_values, *rest,
):
    if shift:
        own_values, out, columns, loads, high, low, acc = rest
    else:
        out, columns, loads, high, low, acc = rest
    lanes = lax.broadcasted_iota(jnp.int32, (8, width), 1)

    def prepare(box, carry):
        value = jnp.where(lanes < near_counts[box], stack_rows(near_values, box, width), 0.0)
        top = value.astype(BF16).astype(F32)
        middle = (value - top).astype(BF16).astype(F32)
        terms = [top, middle, value - top - middle, jnp.zeros_like(value)]
        terms = jnp.concatenate(terms, axis=0).astype(BF16)
        loads[2 * box + 1] = terms[:, :LANES]
        loads[2 * box + 2] = terms[:, LANES:]
        return carry

    lax.fori_loop(0, nearby, prepare, 0, unroll=8)
    loads[0] = jnp.zeros(loads.shape[1:], BF16)
    high[...] = jnp.zeros_like(high)
    low[...] = jnp.zeros_like(low)

    def box_rows(box, rows):
        turned = stack_rows(own_points, box, width).T[0:rows]
        for k in range(3):
            columns[k, 0:rows, :] = jnp.broadcast_to(turned[:, k : k + 1], (rows, LANES))
        acc[...] = jnp.zeros_like(acc)

        def add_group(units, slot):
            value = jnp.concatenate([loads[unit] for unit in units], axis=1)
            total = None
            for part in (high, low):
                term = lax.dot_general(
                    value, part[slot, 0:rows, :], (((1,), (1,)), ((), ())),
                    preferred_element_type=F32,
                )
                total = term if total is None else total + term
            acc[:, 0:rows] += total

        def one_group(g, state):
            slot = state[0]
            add_group(state[1:], 1 - slot)
            first = box * slots + g * group
            points = []
            for unit in range(group):
                place = point_ids[first + unit]
                near = place // 2
                lane = pl.multiple_of((place % 2) * LANES, LANES)
                points.append(
                    [near_points[near, pl.ds(k, 1), pl.ds(lane, LANES)] for k in range(3)]
                )
            for j in range(0, rows, STEP):
                own = [columns[k, j : j + STEP, :] for k in range(3)]
                for unit in range(group):
                    squared = None
                    for k in range(3):
                        along = own[k] - points[unit][k]
                        squared = along * along if squared is None else squared + along * along
                    squared = jnp.maximum(squared, 1e-30)
                    distance = squared * lax.rsqrt(squared)
                    falling = jnp.maximum(RADIUS - distance, 0.0)
                    falling = falling * falling
                    phi = falling * falling * (distance + 0.25 * RADIUS)
                    top = phi.astype(BF16)
                    where = pl.ds(unit * LANES, LANES)
                    high[slot, j : j + STEP, where] = top
                    low[slot, j : j + STEP, where] = (phi - top.astype(F32)).astype(BF16)
            return (1 - slot,) + tuple(load_ids[first + unit] for unit in range(group))

        zero = jnp.int32(0)
        state = lax.fori_loop(0, groups[box], one_group, (zero,) * (group + 1))
        add_group(state[1:], 1 - state[0])
        total = (acc[0:8] + (acc[8:16] + acc[16:24])) * scale
        total = jnp.where(lanes < own_counts[box], total, 0.0)[0:3]
        if shift:
            total = total + shift * own_values[box]
        out[box] = total

    def one_box(box, carry):
        chunks = jnp.maximum((own_counts[box] + (CHUNK - 1)) // CHUNK, 2)
        for count in range(2, width // CHUNK + 1):

            @pl.when(chunks == count)
            def _(count=count):
                box_rows(box, count * CHUNK)

        return carry

    lax.fori_loop(0, boxes, one_box, 0)


def unit_lists(ids, live, near_counts, group):
    boxes, slots = ids.shape
    nearby = near_counts.shape[0]
    chosen = ids[:, :, None] == jnp.arange(nearby, dtype=jnp.int32)
    counts = jnp.sum(jnp.where(chosen, near_counts, 0), axis=2)
    used = jnp.arange(slots, dtype=jnp.int32)[None] < live[:, None]
    flags = jnp.stack([used, used & (counts > LANES)], axis=2).reshape(boxes, 2 * slots)
    units = jnp.stack([2 * ids + 1, 2 * ids + 2], axis=2).reshape(boxes, 2 * slots)
    entry = jnp.arange(2 * slots, dtype=jnp.int32)
    before = flags[:, None, :] & (entry[None, :] < entry[:, None])[None]
    place = jnp.where(flags, jnp.sum(before.astype(jnp.int32), axis=2), -1)
    length = -(-2 * slots // group) * group
    target = place[:, None, :] == jnp.arange(length, dtype=jnp.int32)[None, :, None]
    load_ids = jnp.sum(jnp.where(target, units[:, None, :], 0), axis=2)
    point_ids = jnp.where(load_ids > 0, load_ids, load_ids[:, :1]) - 1
    total = jnp.sum(flags.astype(jnp.int32), axis=1)
    return load_ids, point_ids, (total + (group - 1)) // group


def pair_terms(ids, live, own_counts, near_counts, own_points, near_points, near_values, group, scale, shift, own_values=None):
    boxes, slots = ids.shape
    nearby = near_points.shape[0]
    width = own_points.shape[2]
    operands = [own_points, near_points, near_values] + ([own_values] if shift else [])
    smem = pl.BlockSpec(memory_space=pltpu.SMEM)
    work = boxes * slots * width * width
    load_ids, point_ids, groups = unit_lists(ids, live, near_counts, group)
    return pl.pallas_call(
        functools.partial(
            pair_kernel, boxes, nearby, load_ids.shape[1], group, width, scale, shift
        ),
        out_shape=jax.ShapeDtypeStruct((boxes, 3, width), F32),
        in_specs=[smem] * 5 + [vmem()] * len(operands),
        out_specs=vmem(),
        scratch_shapes=[
            pltpu.VMEM((3, width, LANES), F32),
            pltpu.VMEM((2 * nearby + 1, 32, LANES), BF16),
            pltpu.VMEM((2, width, group * LANES), BF16),
            pltpu.VMEM((2, width, group * LANES), BF16),
            pltpu.VMEM((32, width), F32),
        ],
        compiler_params=pltpu.CompilerParams(vmem_limit_bytes=VMEM_BYTES),
        cost_estimate=pl.CostEstimate(flops=20 * work, bytes_accessed=1 << 20, transcendentals=work),
    )(load_ids.reshape(-1), point_ids.reshape(-1), groups, own_counts, near_counts, *operands)


def lane_parts(first, second):
    total = jnp.sum(first * second, axis=0)
    half = total.shape[1] // 2
    return total[:, :half] + total[:, half:]


def gather_sums(devices, gathered, send_sems, recv_sems, me, base):
    copies = []
    for step in range(1, devices):
        target = lax.rem(me + step, devices)
        copies.append(
            send(
                gathered.at[me],
                gathered.at[me],
                send_sems.at[base + step],
                recv_sems.at[base + step],
                target,
            )
        )
    return copies


def whole_sum(gathered, first):
    rows = jnp.sum(gathered[:, first : first + 3, :], axis=0)
    return jnp.sum(rows, axis=1, keepdims=True)


def first_kernel(devices, rhs, image, direction, coefs, landed, gathered, send_sems, recv_sems):
    me = lax.axis_index("row")
    right = lax.rem(me + 1, devices)
    left = lax.rem(me + devices - 1, devices)
    base = rhs[1]
    mine = image[...]
    gathered[me] = jnp.zeros(gathered.shape[1:], F32)
    gathered[me, 0:3] = lane_parts(base, base)
    gathered[me, 3:6] = lane_parts(base, mine)
    gathered[me, 6:9] = lane_parts(mine, mine)
    greet([lax.rem(me + step, devices) for step in range(1, devices)])
    copies = gather_sums(devices, gathered, send_sems, recv_sems, me, 1)
    copies.append(send(image, landed.at[0], send_sems.at[0], recv_sems.at[0], right))
    copies.append(send(image, landed.at[1], send_sems.at[1], recv_sems.at[1], left))
    for copy in copies:
        copy.wait()
    norm = whole_sum(gathered, 0)
    alpha = norm / whole_sum(gathered, 3)
    norm_next = norm - 2.0 * alpha * whole_sum(gathered, 3) + alpha * alpha * whole_sum(gathered, 6)
    beta = norm_next / norm
    coefs[...] = jnp.zeros_like(coefs)
    coefs[0:3] = jnp.broadcast_to(alpha, (3, coefs.shape[1]))
    coefs[3:6] = jnp.broadcast_to(norm_next, (3, coefs.shape[1]))
    direction[0] = (rhs[0] - alpha[None] * landed[0]) + beta[None] * rhs[0]
    direction[1] = (base - alpha[None] * mine) + beta[None] * base
    direction[2] = (rhs[2] - alpha[None] * landed[1]) + beta[None] * rhs[2]


def last_kernel(devices, rhs, image, direction, second, coefs, mapped, residual, gathered, send_sems, recv_sems):
    me = lax.axis_index("row")
    base = rhs[1]
    along = direction[1]
    gathered[me] = jnp.zeros(gathered.shape[1:], F32)
    gathered[me, 0:3] = lane_parts(along, second[...])
    greet([lax.rem(me + step, devices) for step in range(1, devices)])
    for copy in gather_sums(devices, gathered, send_sems, recv_sems, me, -1):
        copy.wait()
    alpha = coefs[0:3, 0:1][None]
    alpha_next = (coefs[3:6, 0:1] / whole_sum(gathered, 0))[None]
    mapped[...] = alpha * base + alpha_next * along
    residual[...] = (base - alpha * image[...]) - alpha_next * second[...]


def body(solid_points, solid_counts, fluid_points, fluid_forces, fluid_counts, ss_pairs, sf_pairs):
    boxes, _, width = solid_points.shape
    fluids = fluid_points.shape[0]
    devices = lax.axis_size("row")
    me = lax.axis_index("row")
    def count_rows(counts):
        rows = -(-counts.shape[0] // (8 * LANES)) * 8
        padded = jnp.zeros((rows * LANES,), F32).at[: counts.shape[0]].set(counts.astype(F32))
        return padded.reshape(rows, LANES)

    parts = [
        solid_points.reshape(-1, LANES),
        fluid_points.reshape(-1, LANES),
        fluid_forces.reshape(-1, LANES),
        count_rows(solid_counts),
        count_rows(fluid_counts),
    ]
    (landed,) = with_halo([jnp.concatenate(parts, axis=0)], devices, 0)
    pieces, first = [], 0
    for part in parts:
        pieces.append(landed[:, first : first + part.shape[0]])
        first += part.shape[0]
    near_solid = pieces[0].reshape(3 * boxes, 3, width)
    near_fluid = pieces[1].reshape(3 * fluids, 3, width)
    near_forces = pieces[2].reshape(3 * fluids, 3, width)
    near_solid_counts = pieces[3].reshape(3, -1)[:, :boxes].reshape(-1).astype(jnp.int32)
    near_fluid_counts = pieces[4].reshape(3, -1)[:, :fluids].reshape(-1).astype(jnp.int32)
    sf_live = jnp.sum((sf_pairs >= 0).astype(jnp.int32), axis=1)
    ss_live = jnp.sum((ss_pairs >= 0).astype(jnp.int32), axis=1)
    sf_ids = jnp.clip(sf_pairs - (me - 1) * fluids, 0, 3 * fluids - 1)
    ss_ids = jnp.clip(ss_pairs - (me - 1) * boxes, 0, 3 * boxes - 1)

    rhs = pair_terms(
        sf_ids, sf_live, solid_counts, near_fluid_counts,
        solid_points, near_fluid, near_forces,
        4, PHI_SCALE / math.sqrt(width), 0.0,
    )
    (near_rhs,) = with_halo([rhs], devices, 1)

    def operate(near, own):
        return pair_terms(
            ss_ids, ss_live, solid_counts, near_solid_counts,
            solid_points, near_solid, near.reshape(3 * boxes, 3, width),
            2, PHI_SCALE / width, DIAGONAL_SHIFT, own,
        )

    image = operate(near_rhs, rhs)
    block = jax.ShapeDtypeStruct((boxes, 3, width), F32)
    direction, coefs = pl.pallas_call(
        functools.partial(first_kernel, devices),
        out_shape=[
            jax.ShapeDtypeStruct((3, boxes, 3, width), F32),
            jax.ShapeDtypeStruct((8, 128), F32),
        ],
        in_specs=[vmem()] * 2,
        out_specs=[vmem()] * 2,
        scratch_shapes=[
            pltpu.VMEM((2, boxes, 3, width), F32),
            pltpu.VMEM((devices, 16, width // 2), F32),
            pltpu.SemaphoreType.DMA((devices + 1,)),
            pltpu.SemaphoreType.DMA((devices + 1,)),
        ],
        compiler_params=pltpu.CompilerParams(collective_id=2, has_side_effects=True),
    )(near_rhs, image)
    second = operate(direction, direction[1])
    return tuple(
        pl.pallas_call(
            functools.partial(last_kernel, devices),
            out_shape=[block, block],
            in_specs=[vmem()] * 5,
            out_specs=[vmem()] * 2,
            scratch_shapes=[
                pltpu.VMEM((devices, 16, width // 2), F32),
                pltpu.SemaphoreType.DMA((devices - 1,)),
                pltpu.SemaphoreType.DMA((devices - 1,)),
            ],
            compiler_params=pltpu.CompilerParams(collective_id=3, has_side_effects=True),
        )(near_rhs, image, direction, second, coefs)
    )


def solution(mesh):
    return jax.shard_map(
        body,
        mesh=mesh,
        in_specs=(
            P(("parts", "row"), None, None),
            P(("parts", "row")),
            P(("parts", "row"), None, None),
            P(("parts", "row"), None, None),
            P(("parts", "row")),
            P(("parts", "row"), None),
            P(("parts", "row"), None),
        ),
        out_specs=(P(("parts", "row"), None, None), P(("parts", "row"), None, None)),
        check_vma=False,
    )
```
